512 devices in a mesh: rep: 8 (over z_hi, x), fsdp: 64 (over z_lo, y, core).
Axes of the slice: x: 4, y: 8, z: 8 (z_hi: 2, z_lo: 4; z = z_hi * 4 + z_lo), core: 2. Of those that a mesh axis runs over, the one named last changes fastest.
Arguments:
- codes: int32 [8, 2, 14336, 128], P('rep', None, 'fsdp'), may hold values from -8 to 7
- exponents: int32 [8, 2, 14336], P('rep', None, 'fsdp'), may hold values from -6 to -3
- global_params: float32 [2, 14336, 128], P(None, 'fsdp'), may hold values from -6 to 6
- momentum: float32 [2, 14336, 128], P(None, 'fsdp'), may hold values from -4 to 4
- local_params: bfloat16 [8, 2, 14336, 128], P('rep', None, 'fsdp'), may hold values from -6 to 6
- fragment: int32 [2], replicated, may hold values from 0 to 1, each once
Outputs:
- inner_layer: bfloat16 [8, 14336, 128], P('rep')
- new_global: float32 [14336, 128], P('fsdp')
- new_momentum: float32 [14336, 128], P('fsdp')
The draws below stay inside these ranges and needn't reach their ends.
Inputs may be any that keep to these rules, and one draw needn't show every extreme that they name: fragment names each of the 2 layers once.
All inputs are finite; a program needn't handle non-finite values.
Results may differ from the reference program's by a relative error of at most 0.001.
Values may be sent and summed in bfloat16 or wider, within the bound.
No kernel may reach another device: no remote copies, remote signals or barrier semaphores. Data moves between devices by JAX's collectives and lax.ppermute only.
A program may use at most 64 MiB of HBM per device.

```python
import jax
import jax.numpy as jnp
from jax import lax

BLOCK = 128
LAYERS = 2
BLOCKS = 14336
REPS = 8


def plant(drawn, key, smallest, top_value):
    shape = drawn.shape
    index_at = [jax.random.randint(jax.random.fold_in(key, axis), (), 0, shape[axis]) for axis in range(len(shape))]
    drawn = drawn.at[tuple(index_at)].set(smallest)
    longest = shape.index(max(shape))
    index_at[longest] = (index_at[longest] + 1) % shape[longest]
    return drawn.at[tuple(index_at)].set(top_value)


def steps_of(key, dims, split, least, top_value):
    def one(axis_at, blocks):
        heights = jax.random.uniform(jax.random.fold_in(jax.random.fold_in(key, 6), axis_at), (blocks,), jnp.float32, least / len(split), top_value / len(split))
        return jnp.repeat(jnp.exp(heights), dims[axis_at] // blocks).reshape((-1,) + (1,) * (len(dims) - axis_at - 1))

    loudness = one(*split[0])
    for cut in split[1:]:
        loudness = loudness * one(*cut)
    return loudness


def scatter_about(own_key, shape, scale, most, cuts=(), held_as=jnp.bfloat16):
    result = jax.random.normal(own_key, shape, jnp.float32) * scale
    if len(cuts) > 0:
        result = steps_of(own_key, shape, cuts, -0.22, 0.18) * result
    return jnp.clip(result, min=-most, max=most).astype(held_as)


def setup_inputs(seed: int = 0) -> dict:
    streams_of = jax.random.split(jax.random.key(seed), 7)
    codes = plant(jax.random.randint(streams_of[0], (REPS, LAYERS, BLOCKS, BLOCK), -8, 8), jax.random.fold_in(streams_of[0], 1), -8, 7).astype(jnp.int32)
    exponents = plant(jax.random.randint(streams_of[1], (REPS, LAYERS, BLOCKS), -6, -2), jax.random.fold_in(streams_of[1], 1), -6, (-2) - 1).astype(jnp.int32)
    global_params = scatter_about(streams_of[2], (LAYERS, BLOCKS, BLOCK), 1.0, 6.0, ((1, 64),), jnp.float32)
    momentum = scatter_about(streams_of[3], (LAYERS, BLOCKS, BLOCK), 0.3, 4.0, ((1, 64),), jnp.float32)
    local_params = scatter_about(streams_of[4], (REPS, LAYERS, BLOCKS, BLOCK), 1.0, 6.0, ((0, 8), (2, 64)))
    fragment = jax.random.permutation(streams_of[5], LAYERS).astype(jnp.int32)
    return dict(codes=codes, exponents=exponents, global_params=global_params, momentum=momentum, local_params=local_params, fragment=fragment)


outer_momentum = 0.9
outer_rate = 0.7
mix_weight = 0.5


def reference(codes, exponents, global_params, momentum, local_params, fragment):
    active = fragment[0].astype(jnp.int32)
    code_sel = lax.dynamic_index_in_dim(codes, active, 1, keepdims=False)
    expo_sel = lax.dynamic_index_in_dim(exponents, active, 1, keepdims=False)
    rep_term = code_sel.astype(jnp.float32) * jnp.exp2(expo_sel.astype(jnp.float32))[:, :, None]
    rep_term = rep_term.astype(jnp.bfloat16).astype(jnp.float32)
    mean_delta = jnp.sum(rep_term, axis=0) / REPS
    mom_sel = lax.dynamic_index_in_dim(momentum, active, 0, keepdims=False)
    glob_sel = lax.dynamic_index_in_dim(global_params, active, 0, keepdims=False)
    new_momentum = outer_momentum * mom_sel + mean_delta
    new_global = glob_sel - outer_rate * (mean_delta + outer_momentum * new_momentum)
    local_sel = lax.dynamic_index_in_dim(local_params, active, 1, keepdims=False)
    inner_layer = (mix_weight * local_sel.astype(jnp.float32) + (1.0 - mix_weight) * new_global[None]).astype(jnp.bfloat16)
    return inner_layer, new_global, new_momentum
```

```python
import jax
import jax.numpy as jnp
from jax import lax
from jax.sharding import PartitionSpec as P

outer_momentum = 0.9
outer_rate = 0.7
mix_weight = 0.5

NX, NZ, NY, NC = 4, 4, 8, 2
LOWEST = -6


def fsdp_index(z, y, c):
    return (z * NY + y % NY) * NC + c


PLACES = [(z, y, c) for z in range(NZ) for y in range(NY) for c in range(NC)]
SIBLING = [(fsdp_index(z, y, c), fsdp_index(z, y, 1 - c)) for z, y, c in PLACES]
RING = [(fsdp_index(z, y, c), fsdp_index(z, y + 1 - 2 * c, c)) for z, y, c in PLACES]
LINE_Z = [[fsdp_index(z, y, c) for z in range(NZ)] for y in range(NY) for c in range(NC)]
RING_X = [[h * NX + x for x in range(NX)] for h in range(2)]
FAR_Z = [(r, (r + NX) % (2 * NX)) for r in range(2 * NX)]


def to_all(block, axis, groups):
    n = len(groups[0])
    copies = jnp.broadcast_to(block[None], (n,) + block.shape)
    return lax.all_to_all(copies, axis, 0, 0, tiled=True, axis_index_groups=groups)


def shards(codes, exponents, global_params, momentum, local_params, fragment):
    active = fragment[0]

    def pick(array):
        return lax.dynamic_index_in_dim(array, active, 0, keepdims=False)

    units = jnp.left_shift(pick(codes[0]), (pick(exponents[0]) - LOWEST)[:, None]).astype(jnp.bfloat16)
    four = jnp.sum(to_all(units, "rep", RING_X).astype(jnp.float32), axis=0).astype(jnp.bfloat16)
    other = lax.ppermute(four, "rep", FAR_Z)
    mean_delta = (four.astype(jnp.float32) + other.astype(jnp.float32)) * (2.0**LOWEST / (2 * NX))
    new_momentum = outer_momentum * pick(momentum) + mean_delta
    new_global = pick(global_params) - outer_rate * (mean_delta + outer_momentum * new_momentum)
    merged = (mix_weight * pick(local_params[0]).astype(jnp.float32) + (1.0 - mix_weight) * new_global).astype(
        jnp.bfloat16
    )

    me = lax.axis_index("fsdp")
    y, c = (me // NC) % NY, me % NC
    rows = merged.shape[0]
    whole = jnp.zeros((NZ, NY, NC, rows, merged.shape[1]), jnp.bfloat16)

    def put(whole, block, y_at, c_at):
        return lax.dynamic_update_slice(whole, block[:, None, None], (0, y_at % NY, c_at, 0, 0))

    def swap(block):
        return lax.ppermute(block, "fsdp", SIBLING)

    def onward(block):
        return lax.ppermute(block, "fsdp", RING)

    own = to_all(merged, "fsdp", LINE_Z)
    twin = swap(own)
    whole = put(whole, own, y, c)
    whole = put(whole, twin, y, 1 - c)
    toward = 1 - 2 * c
    for step in range(1, NY // 2 + 1):
        own = onward(own)
        whole = put(whole, own, y - toward * step + NY, c)
        whole = put(whole, swap(own), y + toward * step + NY, 1 - c)
        if step < NY // 2:
            twin = onward(twin)
            whole = put(whole, twin, y - toward * step + NY, 1 - c)
            whole = put(whole, swap(twin), y + toward * step + NY, c)
    return (whole.reshape(1, -1, whole.shape[-1]), new_global, new_momentum)


def solution(mesh):
    placed = (
        P("rep", None, "fsdp", None),
        P("rep", None, "fsdp"),
        P(None, "fsdp", None),
        P(None, "fsdp", None),
        P("rep", None, "fsdp", None),
        P(),
    )
    return jax.shard_map(
        shards,
        mesh=mesh,
        in_specs=placed,
        out_specs=(P("rep", None, None), P("fsdp", None), P("fsdp", None)),
        check_vma=False,
    )
```

```python
import jax
import jax.numpy as jnp
from jax import lax
from jax.sharding import PartitionSpec as P

outer_momentum = 0.9
outer_rate = 0.7
mix_weight = 0.5

NX, NZ, NY, NC = 4, 4, 8, 2
LOWEST = -6


def fsdp_index(z, y, c):
    return (z * NY + y % NY) * NC + c


PLACES = [(z, y, c) for z in range(NZ) for y in range(NY) for c in range(NC)]
SIBLING = [(fsdp_index(z, y, c), fsdp_index(z, y, 1 - c)) for z, y, c in PLACES]
RING = [(fsdp_index(z, y, c), fsdp_index(z, y + 1 - 2 * c, c)) for z, y, c in PLACES]
RING_2 = [(fsdp_index(z, y, c), fsdp_index(z, y + 2 - 4 * c, c)) for z, y, c in PLACES]
COUNTER = [(b, a) for a, b in RING]
LINE_Z = [[fsdp_index(z, y, c) for z in range(NZ)] for y in range(NY) for c in range(NC)]
RING_X = [[h * NX + x for x in range(NX)] for h in range(2)]
FAR_Z = [(r, (r + NX) % (2 * NX)) for r in range(2 * NX)]


def to_all(block, axis, groups):
    n = len(groups[0]) if groups else lax.axis_size(axis)
    copies = jnp.broadcast_to(block[None], (n,) + block.shape)
    return lax.all_to_all(copies, axis, 0, 0, tiled=True, axis_index_groups=groups)


def shards(codes, exponents, global_params, momentum, local_params, fragment):
    active = fragment[0]

    def pick(array):
        return lax.dynamic_index_in_dim(array, active, 0, keepdims=False)

    units = jnp.left_shift(pick(codes[0]), (pick(exponents[0]) - LOWEST)[:, None]).astype(jnp.bfloat16)
    four = jnp.sum(to_all(units, "rep", RING_X).astype(jnp.float32), axis=0).astype(jnp.bfloat16)
    other = lax.ppermute(four, "rep", FAR_Z)
    mean_delta = (four.astype(jnp.float32) + other.astype(jnp.float32)) * (2.0**LOWEST / (2 * NX))
    new_momentum = outer_momentum * pick(momentum) + mean_delta
    new_global = pick(global_params) - outer_rate * (mean_delta + outer_momentum * new_momentum)
    merged = (mix_weight * pick(local_params[0]).astype(jnp.float32) + (1.0 - mix_weight) * new_global).astype(
        jnp.bfloat16
    )

    me = lax.axis_index("fsdp")
    y, c = (me // NC) % NY, me % NC
    rows = merged.shape[0]
    whole = jnp.zeros((NZ, NY, NC, rows, merged.shape[1]), jnp.bfloat16)

    def put(whole, block, y_at, c_at):
        return lax.dynamic_update_slice(whole, block[:, None, None], (0, y_at % NY, c_at, 0, 0))

    def swap(block):
        return lax.ppermute(block, "fsdp", SIBLING)

    def onward(block, route):
        return lax.ppermute(block, "fsdp", route)

    own = to_all(merged, "fsdp", LINE_Z)
    first, second = [own], [swap(own)]
    for _ in range(1, NY // 2):
        first.append(onward(first[-1], RING))
        second.append(onward(second[-1], RING))
    across = onward(first[3], RING)
    toward = 1 - 2 * c
    whole = put(whole, first[0], y, c)
    whole = put(whole, second[0], y, 1 - c)
    blocks = []
    for step in range(1, NY // 2):
        blocks += [(step, 0, first[step]), (step, 1, second[step])]
    blocks.append((NY // 2, 0, across))
    for group in ((0, 1), (2, 3), (4, 5), (6,)):
        twins = swap(jnp.stack([blocks[i][2] for i in group]))
        for i, twin in zip(group, twins):
            offset, other, block = blocks[i]
            whole = put(whole, block, y - offset * toward + NY, (c + other) % NC)
            whole = put(whole, twin, y + offset * toward + NY, (1 - c + other) % NC)
    return (whole.reshape(1, -1, whole.shape[-1]), new_global, new_momentum)


def solution(mesh):
    placed = (
        P("rep", None, "fsdp", None),
        P("rep", None, "fsdp"),
        P(None, "fsdp", None),
        P(None, "fsdp", None),
        P("rep", None, "fsdp", None),
        P(),
    )
    return jax.shard_map(
        shards,
        mesh=mesh,
        in_specs=placed,
        out_specs=(P("rep", None, None), P("fsdp", None), P("fsdp", None)),
        check_vma=False,
    )
```

```python
import jax
import jax.numpy as jnp
from jax import lax
from jax.sharding import PartitionSpec as P

outer_momentum = 0.9
outer_rate = 0.7
mix_weight = 0.5

NX, NZ, NY, NC = 4, 4, 8, 2
LOWEST = -6


def fsdp_index(z, y, c):
    return (z * NY + y % NY) * NC + c


PLACES = [(z, y, c) for z in range(NZ) for y in range(NY) for c in range(NC)]
SIBLING = [(fsdp_index(z, y, c), fsdp_index(z, y, 1 - c)) for z, y, c in PLACES]
RING = [(fsdp_index(z, y, c), fsdp_index(z, y + 1 - 2 * c, c)) for z, y, c in PLACES]
RING_2 = [(fsdp_index(z, y, c), fsdp_index(z, y + 2 - 4 * c, c)) for z, y, c in PLACES]
COUNTER = [(b, a) for a, b in RING]
LINE_Z = [[fsdp_index(z, y, c) for z in range(NZ)] for y in range(NY) for c in range(NC)]
RING_X = [[h * NX + x for x in range(NX)] for h in range(2)]
FAR_Z = [(r, (r + NX) % (2 * NX)) for r in range(2 * NX)]


def to_all(block, axis, groups):
    n = len(groups[0]) if groups else lax.axis_size(axis)
    copies = jnp.broadcast_to(block[None], (n,) + block.shape)
    return lax.all_to_all(copies, axis, 0, 0, tiled=True, axis_index_groups=groups)


def shards(codes, exponents, global_params, momentum, local_params, fragment):
    active = fragment[0] & 1

    def pick(array):
        return lax.dynamic_index_in_dim(array, active, 0, keepdims=False, allow_negative_indices=False)

    kept_momentum = outer_momentum * pick(momentum)
    kept_global = pick(global_params) - (outer_rate * outer_momentum) * kept_momentum
    kept_merged = mix_weight * pick(local_params[0]).astype(jnp.float32) + (1.0 - mix_weight) * kept_global
    kept_momentum, kept_global, kept_merged = lax.optimization_barrier((kept_momentum, kept_global, kept_merged))
    units = jnp.left_shift(pick(codes[0]), (pick(exponents[0]) - LOWEST)[:, None]).astype(jnp.bfloat16)
    four = jnp.sum(to_all(units, "rep", RING_X).astype(jnp.float32), axis=0).astype(jnp.bfloat16)
    other = lax.ppermute(four, "rep", FAR_Z)
    mean_delta = (four.astype(jnp.float32) + other.astype(jnp.float32)) * (2.0**LOWEST / (2 * NX))
    new_momentum = kept_momentum + mean_delta
    new_global = kept_global - (outer_rate * (1.0 + outer_momentum)) * mean_delta
    merged = (kept_merged - ((1.0 - mix_weight) * outer_rate * (1.0 + outer_momentum)) * mean_delta).astype(jnp.bfloat16)

    me = lax.axis_index("fsdp")
    y, c = (me >> 1) & (NY - 1), me & (NC - 1)
    rows = merged.shape[0]
    whole = jnp.zeros((NZ, NY, NC, rows, merged.shape[1]), jnp.bfloat16)

    def put(whole, block, y_at, c_at):
        at = (0, y_at & (NY - 1), c_at & (NC - 1), 0, 0)
        return lax.dynamic_update_slice(whole, block[:, None, None], at, allow_negative_indices=False)

    def swap(block):
        return lax.ppermute(block, "fsdp", SIBLING)

    def onward(block, route):
        return lax.ppermute(block, "fsdp", route)

    own = to_all(merged, "fsdp", LINE_Z)
    first, second = [own], [swap(own)]
    for _ in range(1, NY // 2):
        first.append(onward(first[-1], RING))
        second.append(onward(second[-1], RING))
    across = onward(first[3], RING)
    toward = 1 - 2 * c
    whole = put(whole, first[0], y, c)
    whole = put(whole, second[0], y, 1 - c)
    blocks = []
    for step in range(1, NY // 2):
        blocks += [(step, 0, first[step]), (step, 1, second[step])]
    blocks.append((NY // 2, 0, across))
    for group in ((0, 1), (2, 3), (4, 5), (6,)):
        twins = swap(jnp.stack([blocks[i][2] for i in group]))
        for i, twin in zip(group, twins):
            offset, other, block = blocks[i]
            whole = put(whole, block, y - offset * toward, c + other)
            whole = put(whole, twin, y + offset * toward, 1 - c + other)
    return (whole.reshape(1, -1, whole.shape[-1]), new_global, new_momentum)


def solution(mesh):
    placed = (
        P("rep", None, "fsdp", None),
        P("rep", None, "fsdp"),
        P(None, "fsdp", None),
        P(None, "fsdp", None),
        P("rep", None, "fsdp", None),
        P(),
    )
    return jax.shard_map(
        shards,
        mesh=mesh,
        in_specs=placed,
        out_specs=(P("rep", None, None), P("fsdp", None), P("fsdp", None)),
        check_vma=False,
    )
```

```python
import jax
import jax.numpy as jnp
from jax import lax
from jax.experimental import pallas as pl
from jax.experimental.pallas import tpu as pltpu
from jax.sharding import PartitionSpec as P

outer_momentum = 0.9
outer_rate = 0.7
mix_weight = 0.5

NX, NZ, NY, NC = 4, 4, 8, 2
LOWEST = -6


def fsdp_index(z, y, c):
    return (z * NY + y % NY) * NC + c


PLACES = [(z, y, c) for z in range(NZ) for y in range(NY) for c in range(NC)]
SIBLING = [(fsdp_index(z, y, c), fsdp_index(z, y, 1 - c)) for z, y, c in PLACES]
RING = [(fsdp_index(z, y, c), fsdp_index(z, y + 1 - 2 * c, c)) for z, y, c in PLACES]
RING_2 = [(fsdp_index(z, y, c), fsdp_index(z, y + 2 - 4 * c, c)) for z, y, c in PLACES]
RING_3 = [(fsdp_index(z, y, c), fsdp_index(z, y + 3 - 6 * c, c)) for z, y, c in PLACES]
COUNTER = [(b, a) for a, b in RING]
LINE_Z = [[fsdp_index(z, y, c) for z in range(NZ)] for y in range(NY) for c in range(NC)]
RING_X = [[h * NX + x for x in range(NX)] for h in range(2)]
FAR_Z = [(r, (r + NX) % (2 * NX)) for r in range(2 * NX)]


def exchange(copies, axis, groups):
    return lax.all_to_all(copies, axis, 0, 0, tiled=True, axis_index_groups=groups)


def units_kernel(codes, exponents, fragment, out, code_rows, scale_rows, which, sems):
    copies = (
        pltpu.make_async_copy(codes.at[0], code_rows, sems.at[0]),
        pltpu.make_async_copy(exponents.at[0], scale_rows, sems.at[1]),
        pltpu.make_async_copy(fragment, which, sems.at[2]),
    )
    for copy in copies:
        copy.start()
    for copy in copies[::-1]:
        copy.wait()
    active = which[0] & 1
    exponent = jnp.where(active == 0, scale_rows[0:1, :], scale_rows[1:2, :])
    scale = jnp.left_shift(1, exponent - LOWEST).astype(jnp.float32)
    column = jnp.transpose(jnp.broadcast_to(scale, (8, scale.shape[1])))[:, 0:1]
    units = (code_rows[active].astype(jnp.float32) * column).astype(out.dtype)
    for n in range(out.shape[0]):
        out[n] = units


def scaled_codes(codes, exponents, fragment):
    layers, rows, lanes = codes.shape[1:]
    anywhere = pl.BlockSpec(memory_space=pl.ANY)
    return pl.pallas_call(
        units_kernel,
        out_shape=jax.ShapeDtypeStruct((NX, rows, lanes), jnp.bfloat16),
        in_specs=[anywhere] * 3,
        out_specs=pl.BlockSpec(memory_space=pltpu.VMEM),
        scratch_shapes=[
            pltpu.VMEM((layers, rows, lanes), jnp.int32),
            pltpu.VMEM((layers, rows), jnp.int32),
            pltpu.SMEM((layers,), jnp.int32),
            pltpu.SemaphoreType.DMA((3,)),
        ],
        cost_estimate=pl.CostEstimate(flops=4 * rows * lanes, bytes_accessed=8 * rows * lanes * layers, transcendentals=0),
    )(codes, exponents, fragment)


def to_all(block, axis, groups):
    n = len(groups[0]) if groups else lax.axis_size(axis)
    copies = jnp.broadcast_to(block[None], (n,) + block.shape)
    return exchange(copies, axis, groups)


def shards(codes, exponents, global_params, momentum, local_params, fragment):
    active = fragment[0] & 1

    def pick(array):
        return lax.dynamic_index_in_dim(array, active, 0, keepdims=False, allow_negative_indices=False)

    units = scaled_codes(codes, exponents, fragment)
    four = jnp.sum(exchange(units, "rep", RING_X).astype(jnp.float32), axis=0).astype(jnp.bfloat16)
    four, momentum, global_params, local_params = lax.optimization_barrier((four, momentum, global_params, local_params))
    other = lax.ppermute(four, "rep", FAR_Z)
    kept_momentum = outer_momentum * pick(momentum)
    kept_global = pick(global_params) - (outer_rate * outer_momentum) * kept_momentum
    kept_merged = mix_weight * pick(local_params[0]).astype(jnp.float32) + (1.0 - mix_weight) * kept_global
    kept_momentum, kept_global, kept_merged = lax.optimization_barrier((kept_momentum, kept_global, kept_merged))
    mean_delta = (four.astype(jnp.float32) + other.astype(jnp.float32)) * (2.0**LOWEST / (2 * NX))
    new_momentum = kept_momentum + mean_delta
    new_global = kept_global - (outer_rate * (1.0 + outer_momentum)) * mean_delta
    merged = (kept_merged - ((1.0 - mix_weight) * outer_rate * (1.0 + outer_momentum)) * mean_delta).astype(jnp.bfloat16)

    me = lax.axis_index("fsdp")
    y, c = (me >> 1) & (NY - 1), me & (NC - 1)
    rows = merged.shape[0]
    whole = jnp.zeros((NZ, NY, NC, rows, merged.shape[1]), jnp.bfloat16)

    def put(whole, block, y_at, c_at):
        at = (0, y_at & (NY - 1), c_at & (NC - 1), 0, 0)
        return lax.dynamic_update_slice(whole, block[:, None, None], at, allow_negative_indices=False)

    def swap(block):
        return lax.ppermute(block, "fsdp", SIBLING)

    def onward(block, route):
        return lax.ppermute(block, "fsdp", route)

    own = to_all(merged, "fsdp", LINE_Z)
    first = [own]
    first.append(onward(first[0], RING))
    first.append(onward(first[0], RING_2))
    first.append(onward(first[2], RING))
    first.append(onward(first[2], RING_2))
    twin = swap(own)
    second = [twin]
    second.append(onward(second[0], RING))
    second.append(onward(second[0], RING_2))
    second.append(onward(second[2], RING))
    toward = 1 - 2 * c
    whole = put(whole, own, y, c)
    whole = put(whole, twin, y, 1 - c)
    blocks = [(step, other, chain[step]) for step in (1, 2, 3) for other, chain in ((0, first), (1, second))]
    blocks.append((4, 0, first[4]))
    for group in ((0, 1, 2), (3, 4), (5, 6)):
        twins = swap(jnp.stack([blocks[i][2] for i in group]))
        for i, other_half in zip(group, twins):
            offset, other, block = blocks[i]
            whole = put(whole, block, y - offset * toward, c + other)
            whole = put(whole, other_half, y + offset * toward, 1 - c + other)
    return (whole.reshape(1, -1, whole.shape[-1]), new_global, new_momentum)


def solution(mesh):
    placed = (
        P("rep", None, "fsdp", None),
        P("rep", None, "fsdp"),
        P(None, "fsdp", None),
        P(None, "fsdp", None),
        P("rep", None, "fsdp", None),
        P(),
    )
    return jax.shard_map(
        shards,
        mesh=mesh,
        in_specs=placed,
        out_specs=(P("rep", None, None), P("fsdp", None), P("fsdp", None)),
        check_vma=False,
    )
```

```python
import jax
import jax.numpy as jnp
from jax import lax
from jax.sharding import PartitionSpec as P

outer_momentum = 0.9
outer_rate = 0.7
mix_weight = 0.5

NX, NZ, NY, NC = 4, 4, 8, 2
LOWEST = -6


def fsdp_index(z, y, c):
    return (z * NY + y % NY) * NC + c


PLACES = [(z, y, c) for z in range(NZ) for y in range(NY) for c in range(NC)]
SIBLING = [(fsdp_index(z, y, c), fsdp_index(z, y, 1 - c)) for z, y, c in PLACES]
RING = [(fsdp_index(z, y, c), fsdp_index(z, y + 1 - 2 * c, c)) for z, y, c in PLACES]
RING_2 = [(fsdp_index(z, y, c), fsdp_index(z, y + 2 - 4 * c, c)) for z, y, c in PLACES]
COUNTER = [(b, a) for a, b in RING]
LINE_Z = [[fsdp_index(z, y, c) for z in range(NZ)] for y in range(NY) for c in range(NC)]
RING_X = [[h * NX + x for x in range(NX)] for h in range(2)]
FAR_Z = [(r, (r + NX) % (2 * NX)) for r in range(2 * NX)]


def to_all(block, axis, groups):
    n = len(groups[0]) if groups else lax.axis_size(axis)
    copies = jnp.broadcast_to(block[None], (n,) + block.shape)
    return lax.all_to_all(copies, axis, 0, 0, tiled=True, axis_index_groups=groups)


def shards(codes, exponents, global_params, momentum, local_params, fragment):
    active = fragment[0] & 1

    def pick(array):
        return lax.dynamic_index_in_dim(array, active, 0, keepdims=False, allow_negative_indices=False)

    units = jnp.left_shift(pick(codes[0]), (pick(exponents[0]) - LOWEST)[:, None]).astype(jnp.bfloat16)
    four = jnp.sum(to_all(units, "rep", RING_X).astype(jnp.float32), axis=0).astype(jnp.bfloat16)
    four, momentum, global_params, local_params = lax.optimization_barrier((four, momentum, global_params, local_params))
    other = lax.ppermute(four, "rep", FAR_Z)
    kept_momentum = outer_momentum * pick(momentum)
    kept_global = pick(global_params) - (outer_rate * outer_momentum) * kept_momentum
    kept_merged = mix_weight * pick(local_params[0]).astype(jnp.float32) + (1.0 - mix_weight) * kept_global
    kept_momentum, kept_global, kept_merged = lax.optimization_barrier((kept_momentum, kept_global, kept_merged))
    mean_delta = (four.astype(jnp.float32) + other.astype(jnp.float32)) * (2.0**LOWEST / (2 * NX))
    new_momentum = kept_momentum + mean_delta
    new_global = kept_global - (outer_rate * (1.0 + outer_momentum)) * mean_delta
    merged = (kept_merged - ((1.0 - mix_weight) * outer_rate * (1.0 + outer_momentum)) * mean_delta).astype(jnp.bfloat16)

    me = lax.axis_index("fsdp")
    y, c = (me >> 1) & (NY - 1), me & (NC - 1)
    rows = merged.shape[0]
    whole = jnp.zeros((NZ, NY, NC, rows, merged.shape[1]), jnp.bfloat16)

    def put(whole, block, y_at, c_at):
        at = (0, y_at & (NY - 1), c_at & (NC - 1), 0, 0)
        return lax.dynamic_update_slice(whole, block[:, None, None], at, allow_negative_indices=False)

    def swap(block):
        return lax.ppermute(block, "fsdp", SIBLING)

    def onward(block, route):
        return lax.ppermute(block, "fsdp", route)

    own = to_all(merged, "fsdp", LINE_Z)
    first = [own]
    first.append(onward(first[0], RING))
    first.append(onward(first[0], RING_2))
    first.append(onward(first[2], RING))
    first.append(onward(first[2], RING_2))
    twin = swap(own)
    second = [twin]
    second.append(onward(second[0], RING))
    second.append(onward(second[0], RING_2))
    second.append(onward(second[2], RING))
    toward = 1 - 2 * c
    whole = put(whole, own, y, c)
    whole = put(whole, twin, y, 1 - c)
    blocks = [(step, other, chain[step]) for step in (1, 2, 3) for other, chain in ((0, first), (1, second))]
    blocks.append((4, 0, first[4]))
    for group in ((0, 1, 2), (3, 4), (5, 6)):
        twins = swap(jnp.stack([blocks[i][2] for i in group]))
        for i, other_half in zip(group, twins):
            offset, other, block = blocks[i]
            whole = put(whole, block, y - offset * toward, c + other)
            whole = put(whole, other_half, y + offset * toward, 1 - c + other)
    return (whole.reshape(1, -1, whole.shape[-1]), new_global, new_momentum)


def solution(mesh):
    placed = (
        P("rep", None, "fsdp", None),
        P("rep", None, "fsdp"),
        P(None, "fsdp", None),
        P(None, "fsdp", None),
        P("rep", None, "fsdp", None),
        P(),
    )
    return jax.shard_map(
        shards,
        mesh=mesh,
        in_specs=placed,
        out_specs=(P("rep", None, None), P("fsdp", None), P("fsdp", None)),
        check_vma=False,
    )
```

```python
import jax
import jax.numpy as jnp
from jax import lax
from jax.experimental import pallas as pl
from jax.experimental.pallas import tpu as pltpu
from jax.sharding import PartitionSpec as P

outer_momentum = 0.9
outer_rate = 0.7
mix_weight = 0.5

NX, NZ, NY, NC = 4, 4, 8, 2
LOWEST = -6


def fsdp_index(z, y, c):
    return (z * NY + y % NY) * NC + c


PLACES = [(z, y, c) for z in range(NZ) for y in range(NY) for c in range(NC)]
SIBLING = [(fsdp_index(z, y, c), fsdp_index(z, y, 1 - c)) for z, y, c in PLACES]
RING = [(fsdp_index(z, y, c), fsdp_index(z, y + 1 - 2 * c, c)) for z, y, c in PLACES]
RING_2 = [(fsdp_index(z, y, c), fsdp_index(z, y + 2 - 4 * c, c)) for z, y, c in PLACES]
RING_3 = [(fsdp_index(z, y, c), fsdp_index(z, y + 3 - 6 * c, c)) for z, y, c in PLACES]
COUNTER = [(b, a) for a, b in RING]
LINE_Z = [[fsdp_index(z, y, c) for z in range(NZ)] for y in range(NY) for c in range(NC)]
RING_X = [[h * NX + x for x in range(NX)] for h in range(2)]
FAR_Z = [(r, (r + NX) % (2 * NX)) for r in range(2 * NX)]


def exchange(copies, axis, groups):
    return lax.all_to_all(copies, axis, 0, 0, tiled=True, axis_index_groups=groups)


def units_kernel(codes, exponents, fragment, out, code_rows, scale_rows, which, sems):
    copies = (
        pltpu.make_async_copy(codes.at[0], code_rows, sems.at[0]),
        pltpu.make_async_copy(exponents.at[0], scale_rows, sems.at[1]),
        pltpu.make_async_copy(fragment, which, sems.at[2]),
    )
    for copy in copies:
        copy.start()
    for copy in copies[::-1]:
        copy.wait()
    active = which[0] & 1
    exponent = jnp.where(active == 0, scale_rows[0:1, :], scale_rows[1:2, :])
    scale = jnp.left_shift(1, exponent - LOWEST).astype(jnp.float32)
    column = jnp.transpose(jnp.broadcast_to(scale, (8, scale.shape[1])))[:, 0:1]
    out[...] = (code_rows[active].astype(jnp.float32) * column).astype(out.dtype)


def scaled_codes(codes, exponents, fragment):
    layers, rows, lanes = codes.shape[1:]
    anywhere = pl.BlockSpec(memory_space=pl.ANY)
    return pl.pallas_call(
        units_kernel,
        out_shape=jax.ShapeDtypeStruct((rows, lanes), jnp.bfloat16),
        in_specs=[anywhere] * 3,
        out_specs=pl.BlockSpec(memory_space=pltpu.VMEM),
        scratch_shapes=[
            pltpu.VMEM((layers, rows, lanes), jnp.int32),
            pltpu.VMEM((layers, rows), jnp.int32),
            pltpu.SMEM((layers,), jnp.int32),
            pltpu.SemaphoreType.DMA((3,)),
        ],
        cost_estimate=pl.CostEstimate(flops=4 * rows * lanes, bytes_accessed=8 * rows * lanes * layers, transcendentals=0),
    )(codes, exponents, fragment)


def to_all(block, axis, groups):
    n = len(groups[0]) if groups else lax.axis_size(axis)
    copies = jnp.broadcast_to(block[None], (n,) + block.shape)
    return exchange(copies, axis, groups)


def shards(codes, exponents, global_params, momentum, local_params, fragment):
    active = fragment[0] & 1

    def pick(array):
        return lax.dynamic_index_in_dim(array, active, 0, keepdims=False, allow_negative_indices=False)

    units = scaled_codes(codes, exponents, fragment)
    four = jnp.sum(to_all(units, "rep", RING_X).astype(jnp.float32), axis=0).astype(jnp.bfloat16)
    four, momentum, global_params, local_params = lax.optimization_barrier((four, momentum, global_params, local_params))
    other = lax.ppermute(four, "rep", FAR_Z)
    kept_momentum = outer_momentum * pick(momentum)
    kept_global = pick(global_params) - (outer_rate * outer_momentum) * kept_momentum
    kept_merged = mix_weight * pick(local_params[0]).astype(jnp.float32) + (1.0 - mix_weight) * kept_global
    kept_momentum, kept_global, kept_merged = lax.optimization_barrier((kept_momentum, kept_global, kept_merged))
    mean_delta = (four.astype(jnp.float32) + other.astype(jnp.float32)) * (2.0**LOWEST / (2 * NX))
    new_momentum = kept_momentum + mean_delta
    new_global = kept_global - (outer_rate * (1.0 + outer_momentum)) * mean_delta
    merged = (kept_merged - ((1.0 - mix_weight) * outer_rate * (1.0 + outer_momentum)) * mean_delta).astype(jnp.bfloat16)

    me = lax.axis_index("fsdp")
    y, c = (me >> 1) & (NY - 1), me & (NC - 1)
    rows = merged.shape[0]
    whole = jnp.zeros((NZ, NY, NC, rows, merged.shape[1]), jnp.bfloat16)

    def put(whole, block, y_at, c_at):
        at = (0, y_at & (NY - 1), c_at & (NC - 1), 0, 0)
        return lax.dynamic_update_slice(whole, block[:, None, None], at, allow_negative_indices=False)

    def swap(block):
        return lax.ppermute(block, "fsdp", SIBLING)

    def onward(block, route):
        return lax.ppermute(block, "fsdp", route)

    own = to_all(merged, "fsdp", LINE_Z)
    first = [own]
    first.append(onward(first[0], RING))
    first.append(onward(first[0], RING_2))
    first.append(onward(first[2], RING))
    first.append(onward(first[2], RING_2))
    twin = swap(own)
    second = [twin]
    second.append(onward(second[0], RING))
    second.append(onward(second[0], RING_2))
    second.append(onward(second[2], RING))
    toward = 1 - 2 * c
    whole = put(whole, own, y, c)
    whole = put(whole, twin, y, 1 - c)
    blocks = [(step, other, chain[step]) for step in (1, 2, 3) for other, chain in ((0, first), (1, second))]
    blocks.append((4, 0, first[4]))
    for group in ((0, 1, 2), (3, 4), (5, 6)):
        twins = swap(jnp.stack([blocks[i][2] for i in group]))
        for i, other_half in zip(group, twins):
            offset, other, block = blocks[i]
            whole = put(whole, block, y - offset * toward, c + other)
            whole = put(whole, other_half, y + offset * toward, 1 - c + other)
    return (whole.reshape(1, -1, whole.shape[-1]), new_global, new_momentum)


def solution(mesh):
    placed = (
        P("rep", None, "fsdp", None),
        P("rep", None, "fsdp"),
        P(None, "fsdp", None),
        P(None, "fsdp", None),
        P("rep", None, "fsdp", None),
        P(),
    )
    return jax.shard_map(
        shards,
        mesh=mesh,
        in_specs=placed,
        out_specs=(P("rep", None, None), P("fsdp", None), P("fsdp", None)),
        check_vma=False,
    )
```
